32 devices in a mesh: seq: 4 (over y, x), shard: 8 (over z, core).
Axes of the slice: x: 2, y: 2, z: 4, core: 2. Of those that a mesh axis runs over, the one named last changes fastest.
Arguments:
- hidden_in: bfloat16 [16, 2048, 768], P('shard', 'seq'), may hold values from -6 to 6
- seq_lengths: int32 [16], P('shard'), may hold values from 1 to 2048, as said below
- w_qkv: bfloat16 [768, 2304], P('shard'), may hold values from -0.21875 to 0.21875
- b_query: bfloat16 [768], P('shard'), may hold values from -1.5 to 1.5
- b_value: bfloat16 [768], P('shard'), may hold values from -0.5 to 0.5
- w_out: bfloat16 [768, 768], P('shard'), may hold values from -6 to 6
- b_out: bfloat16 [768], P('shard'), may hold values from -1 to 1
- ln1_gain: bfloat16 [768], P('shard'), may hold values from 0.5 to 1.5
- ln1_bias: bfloat16 [768], P('shard'), may hold values from -1 to 1
- w_up: bfloat16 [768, 3072], P('shard'), may hold values from -0.21875 to 0.21875
- b_up: bfloat16 [3072], P('shard'), may hold values from -1 to 1
- w_down: bfloat16 [3072, 768], P('shard'), may hold values from -0.109375 to 0.109375
- b_down: bfloat16 [768], P('shard'), may hold values from -1 to 1
- ln2_gain: bfloat16 [768], P('shard'), may hold values from 0.5 to 1.5
- ln2_bias: bfloat16 [768], P('shard'), may hold values from -1 to 1
- cotangent: bfloat16 [16, 2048, 768], P('shard', 'seq'), may hold values from -6 to 6
Outputs:
- output: bfloat16 [16, 2048, 768], P('shard', 'seq')
- grad_input: bfloat16 [16, 2048, 768], P('shard', 'seq')
- grad_w_qkv: float32 [768, 2304], P('shard')
- grad_b_query: float32 [768], P('shard')
- grad_b_value: float32 [768], P('shard')
- grad_w_out: float32 [768, 768], P('shard')
- grad_b_out: float32 [768], P('shard')
- grad_ln1_gain: float32 [768], P('shard')
- grad_ln1_bias: float32 [768], P('shard')
- grad_w_up: float32 [768, 3072], P('shard')
- grad_b_up: float32 [3072], P('shard')
- grad_w_down: float32 [3072, 768], P('shard')
- grad_b_down: float32 [768], P('shard')
- grad_ln2_gain: float32 [768], P('shard')
- grad_ln2_bias: float32 [768], P('shard')
The draws below stay inside these ranges and needn't reach their ends.
Inputs may be any that keep to these rules, and one draw needn't show every extreme that they name: `seq_lengths`: of sequences 2 i and 2 i + 1, at least one has all 2048 positions valid.
All inputs are finite; a program needn't handle non-finite values.
Results may differ from the reference program's by a relative error of at most 0.018.
Values may be sent and summed in bfloat16 or wider, within the bound.
A program may use at most 192 MiB of HBM per device.

```python
from functools import partial
import jax
import jax.numpy as jnp
from jax import lax

D = 768
H = 12
DH = 64
FF = 3072
SEQ_DEV = 2
LEN = 2048
NSEQ = 16


def draw_seq_lengths(key, part):
    pair_count = NSEQ // 2
    chosen = jax.random.randint(jax.random.fold_in(key, 11), (pair_count,), 0, 2)
    others = jax.random.randint(jax.random.fold_in(key, 12), (pair_count,), 1, LEN + 1)
    first_len = jnp.where(chosen == 0, LEN, others)
    second = jnp.where(chosen == 0, others, LEN)
    return jnp.stack([first_len, second], axis=1).reshape(NSEQ).astype(jnp.int32)


def level_of(own_key, dims, cuts, least, top_value):
    def one(position, blocks):
        steps = jax.random.uniform(jax.random.fold_in(jax.random.fold_in(own_key, 6), position), (blocks,), jnp.float32, least / len(cuts), top_value / len(cuts))
        return jnp.repeat(jnp.exp(steps), dims[position] // blocks).reshape((-1,) + (1,) * (len(dims) - position - 1))

    factor_of = one(*cuts[0])
    for cut in cuts[1:]:
        factor_of = factor_of * one(*cut)
    return factor_of


def gaussian(own_key, extent, deviation, most, shards=(), held_as=jnp.bfloat16):
    values = jax.random.normal(own_key, extent, jnp.float32) * deviation
    if len(shards) > 0:
        values = level_of(own_key, extent, shards, -0.22, 0.18) * values
    return jnp.clip(values, min=-most, max=most).astype(held_as)


def setup_inputs(seed: int = 0) -> dict:
    streams_of = jax.random.split(jax.random.key(seed), 17)
    hidden_in = gaussian(streams_of[0], (NSEQ, LEN, D), 1.0, 6.0, ((0, 8), (1, 4)))
    seq_lengths = draw_seq_lengths(jax.random.fold_in(streams_of[16], 71), 0)
    w_qkv = gaussian(streams_of[2], (D, 3 * D), D ** -0.5, 0.21875, ((0, 8),))
    b_query = gaussian(streams_of[3], (D,), 0.3, 1.5, ((0, 8),))
    b_value = gaussian(streams_of[4], (D,), 0.1, 0.5, ((0, 8),))
    w_out = gaussian(streams_of[5], (D, D), (max(1, 3 * D // LEN)) ** -0.5, 6.0, ((0, 8),))
    b_out = gaussian(streams_of[6], (D,), 0.2, 1.0, ((0, 8),))
    ln1_gain = jnp.clip(1.0 + 0.1 * jax.random.normal(streams_of[7], (D,), jnp.float32), 0.5, 1.5).astype(jnp.bfloat16)
    ln1_bias = gaussian(streams_of[8], (D,), 0.2, 1.0, ((0, 8),))
    w_up = gaussian(streams_of[9], (D, FF), D ** -0.5, 0.21875, ((0, 8),))
    b_up = gaussian(streams_of[10], (FF,), 0.2, 1.0, ((0, 8),))
    w_down = gaussian(streams_of[11], (FF, D), FF ** -0.5, 0.109375, ((0, 8),))
    b_down = gaussian(streams_of[12], (D,), 0.2, 1.0, ((0, 8),))
    ln2_gain = jnp.clip(1.0 + 0.1 * jax.random.normal(streams_of[13], (D,), jnp.float32), 0.5, 1.5).astype(jnp.bfloat16)
    ln2_bias = gaussian(streams_of[14], (D,), 0.2, 1.0, ((0, 8),))
    cotangent = gaussian(streams_of[15], (NSEQ, LEN, D), 1.0, 6.0, ((0, 8), (1, 4)))
    return {"hidden_in": hidden_in, "seq_lengths": seq_lengths, "w_qkv": w_qkv, "b_query": b_query, "b_value": b_value, "w_out": w_out, "b_out": b_out, "ln1_gain": ln1_gain, "ln1_bias": ln1_bias, "w_up": w_up, "b_up": b_up, "w_down": w_down, "b_down": b_down, "ln2_gain": ln2_gain, "ln2_bias": ln2_bias, "cotangent": cotangent}


@jax.custom_vjp
def low(v):
    return lax.optimization_barrier(v.astype(jnp.bfloat16)).astype(jnp.float32)

@jax.custom_vjp
def low_back(v):
    return v

def low_keep(v):
    return (low(v), None)

def low_pass(kept, grad):
    return (grad,)

def back_keep(v):
    return (v, None)

def back_low(kept, grad):
    return (low(grad),)
low.defvjp(low_keep, low_pass)
low_back.defvjp(back_keep, back_low)
HIGH = lax.Precision.HIGHEST
EPS = 1e-12
NEG_FILL = -1e+30

def layer_norm(hidden, gain_vec, shift_vec):
    mean_val = lax.optimization_barrier(jnp.mean(hidden, axis=-1, keepdims=True))
    centered = hidden - mean_val
    inv_std = lax.rsqrt(lax.optimization_barrier(jnp.mean(centered * centered, axis=-1, keepdims=True)) + EPS)
    return centered * inv_std * gain_vec + shift_vec

def block_attend(keys_all, values_all, key_valid, query_blk):
    scores = jnp.einsum('bhd,khd->hbk', query_blk, keys_all, precision=HIGH) * DH ** (-0.5)
    scores = jnp.where(key_valid[None, None, :], low_back(scores), NEG_FILL)
    row_max = lax.optimization_barrier(jnp.max(scores, axis=-1, keepdims=True))
    exp_scores = jnp.exp(scores - row_max)
    attn_prob = exp_scores / lax.optimization_barrier(jnp.sum(exp_scores, axis=-1, keepdims=True))
    return jnp.einsum('hbk,khd->bhd', low(attn_prob), values_all, precision=HIGH)

def attend_sequence(qkv_seq, length):
    block_rows = min(512, LEN)
    key_valid = jnp.arange(LEN) < length
    query_blocks = qkv_seq[:, 0].reshape(LEN // block_rows, block_rows, H, DH)
    one_block = jax.checkpoint(partial(block_attend, qkv_seq[:, 1], qkv_seq[:, 2], key_valid))
    out_blocks = lax.map(one_block, query_blocks)
    return out_blocks.reshape(LEN, H * DH)

def forward(params, hidden, lengths):
    w_qkv, b_query, b_value, w_out, b_out, ln1_gain, ln1_bias, w_up, b_up, w_down, b_down, ln2_gain, ln2_bias = params
    seq_count = hidden.shape[0]
    tokens = hidden.reshape(seq_count * LEN, D)
    qkv_bias = jnp.concatenate([b_query, jnp.zeros_like(b_query), b_value])
    qkv_all = low(low_back(jnp.dot(tokens, w_qkv, precision=HIGH) + qkv_bias))
    qkv_all = qkv_all.reshape(seq_count, LEN, 3, H, DH)
    attended_list = []
    for seq_pos in range(seq_count):
        attended_list.append(attend_sequence(qkv_all[seq_pos], lengths[seq_pos]))
    attended = low(low_back(jnp.concatenate(attended_list, axis=0)))
    projected = low_back(jnp.dot(attended, w_out, precision=HIGH) + b_out)
    ln_one = layer_norm(tokens + projected, ln1_gain, ln1_bias)
    pre_act = low_back(jnp.dot(low(ln_one), w_up, precision=HIGH) + b_up)
    act_low = low(jax.nn.gelu(pre_act, approximate=False))
    ffn_out = low_back(jnp.dot(act_low, w_down, precision=HIGH) + b_down)
    result = layer_norm(ln_one + ffn_out, ln2_gain, ln2_bias)
    return result.reshape(seq_count, LEN, D)

def add_trees(first_tree, second_tree):
    return first_tree + second_tree

def reference(hidden_in, seq_lengths, w_qkv, b_query, b_value, w_out, b_out, ln1_gain, ln1_bias, w_up, b_up, w_down, b_down, ln2_gain, ln2_bias, cotangent):
    params = tuple((param_arr.astype(jnp.float32) for param_arr in (w_qkv, b_query, b_value, w_out, b_out, ln1_gain, ln1_bias, w_up, b_up, w_down, b_down, ln2_gain, ln2_bias)))
    step_count = NSEQ // SEQ_DEV
    hidden_steps = hidden_in.astype(jnp.float32).reshape(step_count, SEQ_DEV, LEN, D)
    cot_steps = cotangent.astype(jnp.float32).reshape(step_count, SEQ_DEV, LEN, D)
    len_steps = seq_lengths.reshape(step_count, SEQ_DEV)

    def scan_step(totals, pieces):
        hidden_blk, cot_blk, len_blk = pieces

        def local_forward(param_set, hidden_arr):
            return forward(param_set, hidden_arr, len_blk)
        result, pullback = jax.vjp(local_forward, params, hidden_blk)
        grad_params, grad_hidden = pullback(cot_blk)
        totals = jax.tree.map(add_trees, totals, grad_params)
        return (totals, (result.astype(jnp.bfloat16), grad_hidden.astype(jnp.bfloat16)))
    zero_grads = jax.tree.map(jnp.zeros_like, params)
    totals, (results, grad_hiddens) = lax.scan(scan_step, zero_grads, (hidden_steps, cot_steps, len_steps))
    output = results.reshape(NSEQ, LEN, D)
    grad_input = grad_hiddens.reshape(NSEQ, LEN, D)
    return (output, grad_input, totals[0], totals[1], totals[2], totals[3], totals[4], totals[5], totals[6], totals[7], totals[8], totals[9], totals[10], totals[11], totals[12])
```

```python
import functools

import jax
import jax.numpy as jnp
from jax import lax
from jax.experimental import pallas as pl
from jax.experimental.pallas import tpu as pltpu
from jax.sharding import PartitionSpec as P

DH = 64
BLOCK_Q = 256
VMEM_LIMIT = 50 * 1024 * 1024
LOG2E = 1.4426950408889634
SCALE = DH ** (-0.5)


EPS = 1e-12
NEG_FILL = -1e30
HALF_ROOT = 0.7071067811865476
INV_ROOT_TAU = 0.3989422804014327


def dot_rows(left_op, right_op):
    return lax.dot_general(
        left_op, right_op, (((0,), (0,)), ((), ())), preferred_element_type=jnp.float32
    )


def dot_last(left_op, right_op):
    return lax.dot_general(
        left_op, right_op, (((1,), (1,)), ((), ())), preferred_element_type=jnp.float32
    )


def norm_forward(hidden, gain_vec, shift_vec):
    mean_val = jnp.mean(hidden, axis=-1, keepdims=True)
    centered = hidden - mean_val
    inv_std = lax.rsqrt(jnp.mean(centered * centered, axis=-1, keepdims=True) + EPS)
    normed = centered * inv_std
    return (normed * gain_vec + shift_vec, normed, inv_std)


def norm_backward(grad_out, normed, inv_std, gain_vec):
    grad_gain = jnp.sum(grad_out * normed, axis=0)
    grad_shift = jnp.sum(grad_out, axis=0)
    scaled = grad_out * gain_vec
    grad_in = inv_std * (
        scaled
        - jnp.mean(scaled, axis=-1, keepdims=True)
        - normed * jnp.mean(scaled * normed, axis=-1, keepdims=True)
    )
    return (grad_in, grad_gain, grad_shift)


def gelu_parts(pre_act):
    cdf_val = 0.5 * (1.0 + lax.erf(pre_act * HALF_ROOT))
    pdf_val = jnp.exp(-0.5 * pre_act * pre_act) * INV_ROOT_TAU
    return (pre_act * cdf_val, cdf_val + pre_act * pdf_val)


def split_three(val):
    hi = val.astype(jnp.bfloat16)
    rest = val - hi.astype(jnp.float32)
    mid = rest.astype(jnp.bfloat16)
    low = (rest - mid.astype(jnp.float32)).astype(jnp.bfloat16)
    return hi, mid, low


def lane_index(rows):
    return lax.broadcasted_iota(jnp.int32, (rows, DH), 1)


def pick_lanes(rows, columns):
    lanes = lane_index(rows)
    out = jnp.zeros((rows, DH), jnp.float32)
    for place, column in columns:
        out = jnp.where(lanes == place, column, out)
    return out.astype(jnp.bfloat16)


def build_keys(len_ref, qkv_ref, kx, vx, heads):
    width = heads * DH
    length = len_ref[0]
    groups, pos, _ = qkv_ref.shape
    for g in range(groups):
        rows = lax.broadcasted_iota(jnp.int32, (pos, DH), 0) + g * pos
        fill = jnp.where(rows < length, 0.0, NEG_FILL)
        lanes = lane_index(pos)
        extra = jnp.where(lanes == 0, fill, jnp.where(lanes < 4, 1.0, 0.0)).astype(jnp.bfloat16)
        ones = jnp.where(lanes < 3, 1.0, 0.0).astype(jnp.bfloat16)
        for h in range(heads):
            key = qkv_ref[g, :, width + h * DH : width + (h + 1) * DH]
            val = qkv_ref[g, :, 2 * width + h * DH : 2 * width + (h + 1) * DH]
            kx[h, g * pos : (g + 1) * pos, :] = jnp.concatenate([key, key, key, extra], axis=1)
            vx[h, g * pos : (g + 1) * pos, :] = jnp.concatenate([val, ones], axis=1)


def fwd_kernel(heads, len_ref, qkv_ref, out_ref, lse_ref, kx, vx):
    step = pl.program_id(0)
    pos = qkv_ref.shape[1]
    block = out_ref.shape[1]
    per = pos // block

    @pl.when(step == 0)
    def _():
        build_keys(len_ref, qkv_ref, kx, vx, heads)

    g = step // per
    start = pl.multiple_of((step % per) * block, block)
    query_all = qkv_ref[g, pl.ds(start, block), :]
    outs = []
    lses = []
    for h in range(heads):
        query = query_all[:, h * DH : (h + 1) * DH].astype(jnp.float32) * (SCALE * LOG2E)
        hi, mid, low = split_three(query)
        qx = jnp.concatenate([hi, mid, low, pick_lanes(block, [(0, 1.0)])], axis=1)
        scores = lax.dot_general(
            qx, kx[h], (((1,), (1,)), ((), ())), preferred_element_type=jnp.float32
        )
        row_max = jnp.max(scores, axis=1, keepdims=True)
        prob = jnp.exp2(scores - row_max).astype(jnp.bfloat16)
        both = jnp.dot(prob, vx[h], preferred_element_type=jnp.float32)
        row_sum = both[:, DH : DH + 1]
        outs.append((both[:, :DH] / row_sum).astype(jnp.bfloat16))
        lses.append(row_max + jnp.log2(row_sum))
    out_ref[0] = jnp.concatenate(outs, axis=1)
    lanes = lax.broadcasted_iota(jnp.int32, (block, 128), 1)
    keep = jnp.zeros((block, 128), jnp.float32)
    for h in range(heads):
        keep = jnp.where(lanes == h, lses[h], keep)
    lse_ref[...] = keep


def attend_forward(qkv, length):
    groups, pos, cols = qkv.shape
    heads = (cols // 3) // DH
    full = groups * pos
    block = min(BLOCK_Q, pos)
    per = pos // block
    return pl.pallas_call(
        functools.partial(fwd_kernel, heads),
        grid=(full // block,),
        in_specs=[
            pl.BlockSpec(memory_space=pltpu.SMEM),
            pl.BlockSpec((groups, pos, cols), lambda i: (0, 0, 0)),
        ],
        out_specs=[
            pl.BlockSpec((1, block, heads * DH), lambda i: (i // per, i % per, 0)),
            pl.BlockSpec((block, 128), lambda i: (i, 0)),
        ],
        out_shape=[
            jax.ShapeDtypeStruct((groups, pos, heads * DH), jnp.bfloat16),
            jax.ShapeDtypeStruct((full, 128), jnp.float32),
        ],
        scratch_shapes=[
            pltpu.VMEM((heads, full, 4 * DH), jnp.bfloat16),
            pltpu.VMEM((heads, full, 2 * DH), jnp.bfloat16),
        ],
        compiler_params=pltpu.CompilerParams(vmem_limit_bytes=VMEM_LIMIT),
        cost_estimate=pl.CostEstimate(
            flops=heads * full * full * 4 * DH * 4,
            bytes_accessed=groups * pos * cols * 2,
            transcendentals=heads * full * full,
        ),
    )(length, qkv)


def bwd_kernel(heads, len_ref, qkv_ref, grad_ref, att_ref, lse_ref, out_ref, kx, vx, dk, dv):
    step = pl.program_id(0)
    steps = pl.num_programs(0)
    groups, pos, cols = qkv_ref.shape
    block = lse_ref.shape[0]
    per = pos // block
    width = heads * DH

    @pl.when(step == 0)
    def _():
        build_keys(len_ref, qkv_ref, kx, vx, heads)
        dk[...] = jnp.zeros_like(dk)
        dv[...] = jnp.zeros_like(dv)

    g = step // per
    start = pl.multiple_of((step % per) * block, block)
    query_all = qkv_ref[g, pl.ds(start, block), :]
    grad_all = grad_ref[g, pl.ds(start, block), :]
    att_all = att_ref[g, pl.ds(start, block), :]
    outs = []
    for h in range(heads):
        raw = query_all[:, h * DH : (h + 1) * DH]
        hi, mid, low = split_three(raw.astype(jnp.float32) * (SCALE * LOG2E))
        a, b, c = split_three(-lse_ref[:, h : h + 1])
        f32 = jnp.float32
        extra = pick_lanes(
            block, [(0, 1.0), (1, a.astype(f32)), (2, b.astype(f32)), (3, c.astype(f32))]
        )
        qx = jnp.concatenate([hi, mid, low, extra], axis=1)
        grad = grad_all[:, h * DH : (h + 1) * DH]
        att = att_all[:, h * DH : (h + 1) * DH]
        row_dot = jnp.sum(grad.astype(f32) * att.astype(f32), axis=1, keepdims=True)
        a, b, c = split_three(-row_dot)
        extra = pick_lanes(block, [(0, a.astype(f32)), (1, b.astype(f32)), (2, c.astype(f32))])
        gx = jnp.concatenate([grad, extra], axis=1)
        prob = jnp.exp2(
            lax.dot_general(kx[h], qx, (((1,), (1,)), ((), ())), preferred_element_type=f32)
        )
        diff = lax.dot_general(vx[h], gx, (((1,), (1,)), ((), ())), preferred_element_type=f32)
        grad_scores = (prob * diff).astype(jnp.bfloat16)
        dv[h] += jnp.dot(prob.astype(jnp.bfloat16), grad, preferred_element_type=f32)
        dk[h] += jnp.dot(grad_scores, raw, preferred_element_type=f32)
        grad_query = lax.dot_general(
            grad_scores, kx[h, :, :DH], (((0,), (0,)), ((), ())), preferred_element_type=f32
        )
        outs.append((grad_query * SCALE).astype(jnp.bfloat16))
    out_ref[g, pl.ds(start, block), 0:width] = jnp.concatenate(outs, axis=1)

    @pl.when(step == steps - 1)
    def _():
        for p in range(groups):
            rows = slice(p * pos, (p + 1) * pos)
            parts = [(dk[h, rows, :] * SCALE).astype(jnp.bfloat16) for h in range(heads)]
            parts += [dv[h, rows, :].astype(jnp.bfloat16) for h in range(heads)]
            if cols > 3 * width:
                parts.append(jnp.zeros((pos, cols - 3 * width), jnp.bfloat16))
            out_ref[p, :, width:] = jnp.concatenate(parts, axis=1)


def attend_backward(qkv, grad, att, lse, length):
    groups, pos, cols = qkv.shape
    heads = (cols // 3) // DH
    full = groups * pos
    block = min(BLOCK_Q, pos)
    whole = lambda last: pl.BlockSpec((groups, pos, last), lambda i: (0, 0, 0))
    return pl.pallas_call(
        functools.partial(bwd_kernel, heads),
        grid=(full // block,),
        in_specs=[
            pl.BlockSpec(memory_space=pltpu.SMEM),
            whole(cols),
            whole(heads * DH),
            whole(heads * DH),
            pl.BlockSpec((block, 128), lambda i: (i, 0)),
        ],
        out_specs=whole(cols),
        out_shape=jax.ShapeDtypeStruct((groups, pos, cols), jnp.bfloat16),
        scratch_shapes=[
            pltpu.VMEM((heads, full, 4 * DH), jnp.bfloat16),
            pltpu.VMEM((heads, full, 2 * DH), jnp.bfloat16),
            pltpu.VMEM((heads, full, DH), jnp.float32),
            pltpu.VMEM((heads, full, DH), jnp.float32),
        ],
        compiler_params=pltpu.CompilerParams(vmem_limit_bytes=VMEM_LIMIT),
        cost_estimate=pl.CostEstimate(
            flops=heads * full * full * 4 * DH * 10,
            bytes_accessed=groups * pos * cols * 4,
            transcendentals=heads * full * full,
        ),
    )(length, qkv, grad, att, lse)


def project_kernel(tok_ref, weight_ref, bias_ref, out_ref):
    out_ref[0] = (
        jnp.dot(tok_ref[...], weight_ref[...], preferred_element_type=jnp.float32) + bias_ref[...]
    ).astype(jnp.bfloat16)


def project_groups(tokens, weight, bias, groups):
    rows, depth = tokens.shape
    cols = weight.shape[1] // groups
    return pl.pallas_call(
        project_kernel,
        grid=(groups,),
        in_specs=[
            pl.BlockSpec((rows, depth), lambda g: (0, 0)),
            pl.BlockSpec((depth, cols), lambda g: (0, g)),
            pl.BlockSpec((1, cols), lambda g: (0, g)),
        ],
        out_specs=pl.BlockSpec((1, rows, cols), lambda g: (g, 0, 0)),
        out_shape=jax.ShapeDtypeStruct((groups, rows, cols), jnp.bfloat16),
        compiler_params=pltpu.CompilerParams(vmem_limit_bytes=VMEM_LIMIT),
        cost_estimate=pl.CostEstimate(
            flops=2 * rows * depth * cols * groups,
            bytes_accessed=2 * (rows * depth + depth * cols * groups + rows * cols * groups),
            transcendentals=0,
        ),
    )(tokens, weight, bias)


def input_grad_kernel(gq_ref, weight_ref, base_ref, out_ref):
    groups, _, cols = gq_ref.shape
    total = base_ref[...]
    for g in range(groups):
        total += lax.dot_general(
            gq_ref[g],
            weight_ref[:, g * cols : (g + 1) * cols],
            (((1,), (1,)), ((), ())),
            preferred_element_type=jnp.float32,
        )
    out_ref[...] = total.astype(jnp.bfloat16)


def input_grad(grad_qkv, weight, base):
    groups, rows, cols = grad_qkv.shape
    depth = weight.shape[0]
    block = min(256, rows)
    return pl.pallas_call(
        input_grad_kernel,
        grid=(rows // block,),
        in_specs=[
            pl.BlockSpec((groups, block, cols), lambda i: (0, i, 0)),
            pl.BlockSpec(weight.shape, lambda i: (0, 0)),
            pl.BlockSpec((block, depth), lambda i: (i, 0)),
        ],
        out_specs=pl.BlockSpec((block, depth), lambda i: (i, 0)),
        out_shape=jax.ShapeDtypeStruct((rows, depth), jnp.bfloat16),
        compiler_params=pltpu.CompilerParams(vmem_limit_bytes=VMEM_LIMIT),
        cost_estimate=pl.CostEstimate(
            flops=2 * rows * depth * cols * groups,
            bytes_accessed=2 * (3 * rows * depth + depth * cols * groups + rows * cols * groups),
            transcendentals=0,
        ),
    )(grad_qkv, weight, base)


def swap_groups(arr):
    return lax.all_to_all(arr, "seq", split_axis=0, concat_axis=0, tiled=True)


def sum_groups(share):
    groups = lax.axis_size("seq")
    if groups != 4:
        return jnp.sum(lax.all_gather(share, "seq", axis=0).astype(jnp.float32), axis=0)
    others = [
        lax.ppermute(share, "seq", [(i, i ^ k) for i in range(groups)]).astype(jnp.float32)
        for k in (1, 2, 3)
    ]
    return (share.astype(jnp.float32) + others[0]) + (others[1] + others[2])


def reduce_rows(grad):
    share = lax.psum_scatter(grad.astype(jnp.bfloat16), "shard", scatter_dimension=0, tiled=True)
    return sum_groups(share)


def reduce_with(grad, vectors):
    rows = grad.shape[0]
    columns = jnp.concatenate([vec.reshape(rows, -1) for vec in vectors], axis=1)
    columns = jnp.pad(columns, ((0, 0), (0, -columns.shape[1] % 128)))
    total = reduce_rows(jnp.concatenate([grad, columns], axis=1))
    outs = [total[:, : grad.shape[1]]]
    start = grad.shape[1]
    for vec in vectors:
        count = vec.shape[0] // rows
        outs.append(total[:, start : start + count].reshape(-1))
        start += count
    return outs


def per_device(
    hidden_in,
    seq_lengths,
    w_qkv,
    b_query,
    b_value,
    w_out,
    b_out,
    ln1_gain,
    ln1_bias,
    w_up,
    b_up,
    w_down,
    b_down,
    ln2_gain,
    ln2_bias,
    cotangent,
):
    groups = lax.axis_size("seq")
    shard_count = lax.axis_size("shard")
    seq_count, pos, model_width = hidden_in.shape
    tok_count = seq_count * pos
    width = model_width // groups
    cols = -(-3 * width // 128) * 128
    f32 = jnp.float32
    small = (b_query, b_value, b_out, ln1_gain, ln1_bias, b_down, ln2_gain, ln2_bias, b_up)
    packed = lax.all_gather(jnp.concatenate(small), "shard", axis=0)
    full_small = []
    start = 0
    for vec in small:
        full_small.append(packed[:, start : start + vec.shape[0]].reshape(-1).astype(f32))
        start += vec.shape[0]
    (
        query_bias,
        value_bias,
        out_bias,
        gain_one,
        shift_one,
        down_bias,
        gain_two,
        shift_two,
        up_bias,
    ) = full_small
    by_group = jnp.swapaxes(w_qkv.reshape(w_qkv.shape[0], 3, groups, width), 1, 2).reshape(
        w_qkv.shape[0], groups, 3 * width
    )
    by_group = jnp.pad(by_group, ((0, 0), (0, 0), (0, cols - 3 * width)))
    qkv_weight = lax.all_gather(
        by_group.reshape(w_qkv.shape[0], groups * cols), "shard", axis=0, tiled=True
    )
    out_weight = lax.all_gather(w_out, "shard", axis=0, tiled=True)
    up_weight = lax.all_gather(w_up, "shard", axis=0, tiled=True)
    down_weight = lax.all_gather(w_down, "shard", axis=0, tiled=True)
    bias = jnp.stack([query_bias, jnp.zeros_like(query_bias), value_bias])
    bias = jnp.swapaxes(bias.reshape(3, groups, width), 0, 1).reshape(groups, 3 * width)
    bias = jnp.pad(bias, ((0, 0), (0, cols - 3 * width))).reshape(1, groups * cols)
    tokens = hidden_in.reshape(tok_count, model_width)
    lengths = [seq_lengths[n : n + 1] for n in range(seq_count)]
    qkv = [
        swap_groups(project_groups(hidden_in[n], qkv_weight, bias, groups))
        for n in range(seq_count)
    ]
    att = []
    lse = []
    arrived = []
    for n in range(seq_count):
        att_n, lse_n = attend_forward(qkv[n], lengths[n])
        att.append(att_n)
        lse.append(lse_n)
        arrived.append(swap_groups(att_n))
    attended = jnp.concatenate(
        [jnp.swapaxes(arr, 0, 1).reshape(pos, model_width) for arr in arrived]
    )
    projected = jnp.dot(attended, out_weight, preferred_element_type=f32) + out_bias
    ln_one, normed_one, inv_one = norm_forward(
        tokens.astype(f32) + projected, gain_one, shift_one
    )
    ln_low = ln_one.astype(jnp.bfloat16)
    pre_act = jnp.dot(ln_low, up_weight, preferred_element_type=f32) + up_bias
    act_val, act_slope = gelu_parts(pre_act)
    act_low = act_val.astype(jnp.bfloat16)
    ffn_out = jnp.dot(act_low, down_weight, preferred_element_type=f32) + down_bias
    result, normed_two, inv_two = norm_forward(ln_one + ffn_out, gain_two, shift_two)
    output = result.astype(jnp.bfloat16).reshape(seq_count, pos, model_width)
    grad_y = cotangent.reshape(tok_count, model_width).astype(f32)
    grad_two, grad_gain_two, grad_shift_two = norm_backward(grad_y, normed_two, inv_two, gain_two)
    grad_ffn = grad_two.astype(jnp.bfloat16)
    grad_down_bias = jnp.sum(grad_ffn, axis=0, dtype=f32)
    grad_down = reduce_rows(dot_rows(act_low, grad_ffn))
    grad_pre = (dot_last(grad_ffn, down_weight) * act_slope).astype(jnp.bfloat16)
    grad_up_bias = jnp.sum(grad_pre, axis=0, dtype=f32)
    grad_up = reduce_rows(dot_rows(ln_low, grad_pre))
    grad_ln = dot_last(grad_pre, up_weight) + grad_two
    grad_one, grad_gain_one, grad_shift_one = norm_backward(grad_ln, normed_one, inv_one, gain_one)
    grad_proj = grad_one.astype(jnp.bfloat16)
    grad_out_bias = jnp.sum(grad_proj, axis=0, dtype=f32)
    (
        grad_out,
        sum_out_bias,
        sum_gain_one,
        sum_shift_one,
        sum_down_bias,
        sum_gain_two,
        sum_shift_two,
        sum_up_bias,
    ) = reduce_with(
        dot_rows(attended, grad_proj),
        (
            grad_out_bias,
            grad_gain_one,
            grad_shift_one,
            grad_down_bias,
            grad_gain_two,
            grad_shift_two,
            grad_up_bias,
        ),
    )
    grad_att = dot_last(grad_proj, out_weight).astype(jnp.bfloat16)
    grad_att = grad_att.reshape(seq_count, pos, groups, width)
    grad_heads = [swap_groups(jnp.swapaxes(grad_att[n], 0, 1)) for n in range(seq_count)]
    back = [
        swap_groups(attend_backward(qkv[n], grad_heads[n], att[n], lse[n], lengths[n]))
        for n in range(seq_count)
    ]
    grad_base = grad_one.reshape(seq_count, pos, model_width)
    grad_input = jnp.stack(
        [input_grad(back[n], qkv_weight, grad_base[n]) for n in range(seq_count)]
    )
    grad_qkv = jnp.concatenate(back, axis=1)[:, :, : 3 * width]
    by_part = [dot_rows(tokens, grad_qkv[g]) for g in range(groups)]
    grad_w = jnp.stack(by_part, axis=1).reshape(model_width, groups, 3, width)
    grad_w = jnp.swapaxes(grad_w, 1, 2).reshape(model_width, 3 * model_width)
    col_sum = jnp.sum(grad_qkv, axis=1, dtype=f32).reshape(groups, 3, width)
    grad_w, sum_query_bias, sum_value_bias = reduce_with(
        grad_w, (col_sum[:, 0].reshape(-1), col_sum[:, 2].reshape(-1))
    )
    return (
        output,
        grad_input,
        grad_w,
        sum_query_bias,
        sum_value_bias,
        grad_out,
        sum_out_bias,
        sum_gain_one,
        sum_shift_one,
        grad_up,
        sum_up_bias,
        grad_down,
        sum_down_bias,
        sum_gain_two,
        sum_shift_two,
    )


def solution(mesh):
    in_specs = (
        P("shard", "seq", None),
        P("shard"),
        P("shard", None),
        P("shard"),
        P("shard"),
        P("shard", None),
        P("shard"),
        P("shard"),
        P("shard"),
        P("shard", None),
        P("shard"),
        P("shard", None),
        P("shard"),
        P("shard"),
        P("shard"),
        P("shard", "seq", None),
    )
    out_specs = (
        P("shard", "seq", None),
        P("shard", "seq", None),
        P("shard", None),
        P("shard"),
        P("shard"),
        P("shard", None),
        P("shard"),
        P("shard"),
        P("shard"),
        P("shard", None),
        P("shard"),
        P("shard", None),
        P("shard"),
        P("shard"),
        P("shard"),
    )
    return jax.shard_map(
        per_device, mesh=mesh, in_specs=in_specs, out_specs=out_specs, check_vma=False
    )
```
